32 devices in a mesh: group: 2 (over y), space: 4 (over z), dp: 2 (over core), mp: 2 (over x).
Axes of the slice: x: 2, y: 2, z: 4, core: 2. Of those that a mesh axis runs over, the one named last changes fastest.
Arguments:
- node_latent: bfloat16 [4, 1024, 512], P(('group', 'dp'), 'space'), parts along dimension 0, may hold values from -6 to 6
- halo_latent: bfloat16 [4, 1024, 512], P(('group', 'dp'), 'space'), parts along dimension 0, may hold values from -6 to 6
- coarse_latent: bfloat16 [4, 32, 512], P(('group', 'dp')), parts along dimension 0, may hold values from -6 to 6
- edge_latent: bfloat16 [4, 2048, 512], P(('group', 'dp'), 'space'), parts along dimension 0, may hold values from -6 to 6
- edge_preact: bfloat16 [4, 2048, 512], P(('group', 'dp'), 'space', 'mp'), parts along dimension 0, may hold values from -6 to 6
- edge_mixed: bfloat16 [4, 2048, 512], P(('group', 'dp'), 'space'), parts along dimension 0, may hold values from -6 to 6
- node_message: bfloat16 [4, 1024, 512], P(('group', 'dp'), 'space'), parts along dimension 0, may hold values from -12 to 12
- node_preact: bfloat16 [4, 1024, 512], P(('group', 'dp'), 'space', 'mp'), parts along dimension 0, may hold values from -6 to 6
- node_mixed: bfloat16 [4, 1024, 512], P(('group', 'dp'), 'space'), parts along dimension 0, may hold values from -6 to 6
- edge_cotangent: bfloat16 [4, 2048, 512], P(('group', 'dp'), 'space'), parts along dimension 0, may hold values from -6 to 6
- node_cotangent: bfloat16 [4, 1024, 512], P(('group', 'dp'), 'space'), parts along dimension 0, may hold values from -6 to 6
- senders: int32 [2048], P('space'), may hold values from 0 to 543
- receivers: int32 [2048], P('space'), may hold values from 0 to 255
- send_rows: int32 [4, 2, 128], P('space'), may hold values from 0 to 255
- coarse_rows: int32 [32], replicated, may hold values from 0 to 255
- edge_up: bfloat16 [1536, 512], P(None, 'mp'), may hold values from -0.15625 to 0.15625
- edge_down: bfloat16 [512, 512], P('mp'), may hold values from -0.25 to 0.25
- edge_gain: float32 [512], replicated, may hold values from 0.1 to 1.9
- node_up: bfloat16 [1024, 512], P(None, 'mp'), may hold values from -0.1875 to 0.1875
- node_down: bfloat16 [512, 512], P('mp'), may hold values from -0.25 to 0.25
- node_gain: float32 [512], replicated, may hold values from 0.1 to 1.9
Outputs:
- node_grad: bfloat16 [4, 1024, 512], P(('group', 'dp'), 'space', 'mp'), parts along dimension 0
- edge_grad: bfloat16 [4, 2048, 512], P(('group', 'dp'), 'space', 'mp'), parts along dimension 0
- edge_upgrad: bfloat16 [3072, 512], P('group', 'mp'), parts along dimension 0
- edge_downgrad: bfloat16 [1024, 512], P(('group', 'mp')), parts along dimension 0
- node_upgrad: bfloat16 [2048, 512], P('group', 'mp'), parts along dimension 0
- node_downgrad: bfloat16 [1024, 512], P(('group', 'mp')), parts along dimension 0
- edge_gaingrad: float32 [1024], P('group'), parts along dimension 0
- node_gaingrad: float32 [1024], P('group'), parts along dimension 0
The draws below stay inside these ranges and needn't reach their ends.
There are 2 independent parts, one for each index of `group`. The reference program is written for one: setup_inputs(seed, part) draws one part's arguments, and reference() takes and returns one part's arrays. A program takes and returns all parts, laid end to end along the dimension named above; an argument that names none is the same for every part. Nothing has to cross between parts.
Inputs may be any that keep to these rules, and one draw needn't show every extreme that they name: `senders`: a row of the edge's region's extended table. `receivers`: a row among the edge's region's own nodes. `send_rows`: rows among the sending region's own nodes. `coarse_rows`: coarse node c is owned by region c // 8; the entry is a row among that region's own nodes, below 256.
All inputs are finite; a program needn't handle non-finite values.
Results may differ from the reference program's by a relative error of at most 0.015.
Values may be sent and summed in bfloat16 or wider, within the bound.
A program may use at most 64 MiB of HBM per device.

```python
import math
import jax
import jax.numpy as jnp
from jax import lax

D = 512
H = 512
NODE_DEV = 256
EDGE_DEV = 512
COARSE_DEV = 8
HALO = 128
SAMPLES = 2
REGIONS = 4
NODES = 1024
EDGES = 2048
COARSE = 32
EXTENDED = 544


def touch_ends(entries, stream_key, smallest, high):
    place = [jax.random.randint(jax.random.fold_in(stream_key, axis), (), 0, length) for axis, length in enumerate(entries.shape)]
    main_axis = entries.shape.index(max(entries.shape))
    beside = place[:main_axis] + [(place[main_axis] + 1) % entries.shape[main_axis]] + place[main_axis + 1:]
    return entries.at[tuple(place)].set(smallest).at[tuple(beside)].set(high)


def block_levels(stream_key, extent, split, least, top_value):
    loudness, own = 1.0, jax.random.fold_in(stream_key, 6)
    for dim, shards_of in split:
        steps = jnp.exp(jax.random.uniform(jax.random.fold_in(own, dim), (shards_of,), jnp.float32, least / len(split), top_value / len(split)))
        loudness = loudness * jnp.repeat(steps, extent[dim] // shards_of).reshape([-1 if axis == dim else 1 for axis in range(len(extent))])
    return loudness


def normal_values(stream_key, dims, spread, limit, cuts=(), held_as=jnp.bfloat16):
    loudness = block_levels(stream_key, dims, cuts, -0.22, 0.18) if cuts else 1.0
    array = jax.random.normal(stream_key, dims, jnp.float32) * spread * loudness
    return jnp.minimum(jnp.maximum(array, -limit), limit).astype(held_as)


def setup_inputs(seed: int = 0, part: int = 0) -> dict:
    streams_of = jax.random.split(jax.random.key(seed), 22)
    part_splits = jax.random.split(jax.random.fold_in(streams_of[21], part), 22)
    node_latent = normal_values(part_splits[0], (SAMPLES, NODES, D), 1.0, 6.0, ((0, 2), (1, 4)))
    halo_latent = normal_values(part_splits[1], (SAMPLES, REGIONS * 2 * HALO, D), 1.0, 6.0, ((0, 2), (1, 4)))
    coarse_latent = normal_values(part_splits[2], (SAMPLES, COARSE, D), 1.0, 6.0, ((0, 2),))
    edge_latent = normal_values(part_splits[3], (SAMPLES, EDGES, D), 1.0, 6.0, ((0, 2), (1, 4)))
    edge_preact = normal_values(part_splits[4], (SAMPLES, EDGES, H), 1.5, 6.0, ((0, 2), (1, 4), (2, 2)))
    edge_mixed = normal_values(part_splits[5], (SAMPLES, EDGES, D), 1.0, 6.0, ((0, 2), (1, 4)))
    node_message = normal_values(part_splits[6], (SAMPLES, NODES, D), 2.0, 12.0, ((0, 2), (1, 4)))
    node_preact = normal_values(part_splits[7], (SAMPLES, NODES, H), 1.5, 6.0, ((0, 2), (1, 4), (2, 2)))
    node_mixed = normal_values(part_splits[8], (SAMPLES, NODES, D), 1.0, 6.0, ((0, 2), (1, 4)))
    edge_cotangent = normal_values(part_splits[9], (SAMPLES, EDGES, D), 1.0, 6.0, ((0, 2), (1, 4)))
    node_cotangent = normal_values(part_splits[10], (SAMPLES, NODES, D), 1.0, 6.0, ((0, 2), (1, 4)))
    senders = touch_ends(jax.random.randint(streams_of[11], (EDGES,), 0, EXTENDED), jax.random.fold_in(streams_of[11], 1), 0, EXTENDED - 1).astype(jnp.int32)
    receivers = touch_ends(jax.random.randint(streams_of[12], (EDGES,), 0, NODE_DEV), jax.random.fold_in(streams_of[12], 1), 0, NODE_DEV - 1).astype(jnp.int32)
    send_rows = touch_ends(jax.random.randint(streams_of[13], (REGIONS, 2, HALO), 0, NODE_DEV), jax.random.fold_in(streams_of[13], 1), 0, NODE_DEV - 1).astype(jnp.int32)
    coarse_rows = touch_ends(jax.random.randint(streams_of[14], (COARSE,), 0, NODE_DEV), jax.random.fold_in(streams_of[14], 1), 0, NODE_DEV - 1).astype(jnp.int32)
    edge_up = normal_values(streams_of[15], (3 * D, H), (3 * D) ** -0.5, 0.15625, ((1, 2),))
    edge_down = normal_values(streams_of[16], (H, D), H ** -0.5, 0.25, ((0, 2),))
    edge_gain = jnp.clip(1.0 + 0.18 * jax.random.normal(streams_of[17], (D,), jnp.float32), 0.1, 1.9)
    node_up = normal_values(streams_of[18], (2 * D, H), (2 * D) ** -0.5, 0.1875, ((1, 2),))
    node_down = normal_values(streams_of[19], (H, D), H ** -0.5, 0.25, ((0, 2),))
    node_gain = jnp.clip(1.0 + 0.18 * jax.random.normal(streams_of[20], (D,), jnp.float32), 0.1, 1.9)
    return dict(node_latent=node_latent, halo_latent=halo_latent, coarse_latent=coarse_latent, edge_latent=edge_latent, edge_preact=edge_preact, edge_mixed=edge_mixed, node_message=node_message, node_preact=node_preact, node_mixed=node_mixed, edge_cotangent=edge_cotangent, node_cotangent=node_cotangent, senders=senders, receivers=receivers, send_rows=send_rows, coarse_rows=coarse_rows, edge_up=edge_up, edge_down=edge_down, edge_gain=edge_gain, node_up=node_up, node_down=node_down, node_gain=node_gain)


EPSILON = 1e-05

def silu_slope(preact):
    logistic = jax.nn.sigmoid(preact)
    return logistic * (1.0 + preact * (1.0 - logistic))

def norm_back(mixed, norm_gain, upstream):
    values = mixed.astype(jnp.float32)
    centred = values - lax.optimization_barrier(jnp.mean(values, -1, keepdims=True))
    inverse = lax.rsqrt(lax.optimization_barrier(jnp.mean(centred * centred, -1, keepdims=True)) + EPSILON)
    normed = centred * inverse
    scaled = upstream * norm_gain
    mix_delta = inverse * (scaled - lax.optimization_barrier(jnp.mean(scaled, -1, keepdims=True)) - normed * lax.optimization_barrier(jnp.mean(scaled * normed, -1, keepdims=True)))
    return (mix_delta, normed)

def float_einsum(form, left, right):
    return jnp.einsum(form, left.astype(jnp.float32), right.astype(jnp.float32))

def segment_rows(values, index, count):

    def one_sample(sample_rows):
        return jax.ops.segment_sum(sample_rows, index, count)
    return jax.vmap(one_sample)(values)

def reference(node_latent, halo_latent, coarse_latent, edge_latent, edge_preact, edge_mixed, node_message, node_preact, node_mixed, edge_cotangent, node_cotangent, senders, receivers, send_rows, coarse_rows, edge_up, edge_down, edge_gain, node_up, node_down, node_gain):
    samples = node_latent.shape[0]
    width = node_latent.shape[2]
    node_scale = 1.0 / math.sqrt(SAMPLES * NODES)
    edge_scale = 1.0 / math.sqrt(SAMPLES * EDGES)
    node_upstream = node_cotangent.astype(jnp.float32)
    node_delta, node_normed = norm_back(node_mixed, node_gain, node_upstream)
    node_gaingrad = lax.optimization_barrier(jnp.sum(node_upstream * node_normed, axis=(0, 1))) * node_scale
    node_delta = node_delta.astype(jnp.bfloat16)
    node_act = node_preact.astype(jnp.float32)
    node_hidden = jax.nn.silu(node_act).astype(jnp.bfloat16)
    node_signal = (float_einsum('snd,hd->snh', node_delta, node_down) * silu_slope(node_act)).astype(jnp.bfloat16)
    node_downgrad = (float_einsum('snh,snd->hd', node_hidden, node_delta) * node_scale).astype(jnp.bfloat16)
    node_upgrad = jnp.concatenate([float_einsum('snd,snh->dh', node_latent, node_signal), float_einsum('snd,snh->dh', node_message, node_signal)], 0)
    node_upgrad = (node_upgrad * node_scale).astype(jnp.bfloat16)
    node_terms = float_einsum('snh,ch->snc', node_signal, node_up)
    node_back = node_terms[:, :, :width]
    message_grad = node_terms[:, :, width:]
    region_ids = jnp.arange(REGIONS, dtype=jnp.int32)
    recv_rows = (receivers.reshape(REGIONS, EDGE_DEV) + region_ids[:, None] * NODE_DEV).reshape(-1).astype(jnp.int32)
    send_glob = (senders.reshape(REGIONS, EDGE_DEV) + region_ids[:, None] * EXTENDED).reshape(-1).astype(jnp.int32)
    edge_upstream = edge_cotangent.astype(jnp.float32) + message_grad[:, recv_rows]
    edge_delta, edge_normed = norm_back(edge_mixed, edge_gain, edge_upstream)
    edge_gaingrad = lax.optimization_barrier(jnp.sum(edge_upstream * edge_normed, axis=(0, 1))) * edge_scale
    edge_delta = edge_delta.astype(jnp.bfloat16)
    edge_act = edge_preact.astype(jnp.float32)
    edge_hidden = jax.nn.silu(edge_act).astype(jnp.bfloat16)
    edge_signal = (float_einsum('sed,hd->seh', edge_delta, edge_down) * silu_slope(edge_act)).astype(jnp.bfloat16)
    coarse_copies = jnp.broadcast_to(coarse_latent[:, None], (samples, REGIONS, COARSE, width))
    extended = jnp.concatenate([node_latent.reshape(samples, REGIONS, NODE_DEV, width), halo_latent.reshape(samples, REGIONS, 2 * HALO, width), coarse_copies], 2)
    extended = extended.reshape(samples, REGIONS * EXTENDED, width)
    sender_latent = extended[:, send_glob]
    receiver_latent = node_latent[:, recv_rows]
    edge_upgrad = jnp.concatenate([float_einsum('sed,seh->dh', edge_latent, edge_signal), float_einsum('sed,seh->dh', sender_latent, edge_signal), float_einsum('sed,seh->dh', receiver_latent, edge_signal)], 0)
    edge_upgrad = (edge_upgrad * edge_scale).astype(jnp.bfloat16)
    edge_downgrad = (float_einsum('seh,sed->hd', edge_hidden, edge_delta) * edge_scale).astype(jnp.bfloat16)
    edge_terms = float_einsum('seh,ch->sec', edge_signal, edge_up)
    edge_grad = (edge_cotangent.astype(jnp.float32) + edge_terms[:, :, :width]).astype(jnp.bfloat16)
    sender_part = edge_terms[:, :, width:2 * width]
    receiver_part = edge_terms[:, :, 2 * width:]
    ext_grad = segment_rows(sender_part, send_glob, REGIONS * EXTENDED).reshape(samples, REGIONS, EXTENDED, width)
    node_sum = node_cotangent.astype(jnp.float32) + node_back + segment_rows(receiver_part, recv_rows, NODES)
    node_sum = node_sum + ext_grad[:, :, :NODE_DEV].reshape(samples, NODES, width)
    for slot, offset in enumerate((-1, 1)):
        block = ext_grad[:, :, NODE_DEV + slot * HALO:NODE_DEV + (slot + 1) * HALO]
        moved = jnp.roll(block, offset, axis=1)
        target_rows = (send_rows[:, slot, :] + region_ids[:, None] * NODE_DEV).reshape(-1).astype(jnp.int32)
        node_sum = node_sum.at[:, target_rows].add(moved.reshape(samples, REGIONS * HALO, width))
    coarse_total = lax.optimization_barrier(jnp.sum(ext_grad[:, :, NODE_DEV + 2 * HALO:], axis=1))
    coarse_glob = (jnp.arange(COARSE, dtype=jnp.int32) // COARSE_DEV * NODE_DEV + coarse_rows).astype(jnp.int32)
    node_sum = node_sum.at[:, coarse_glob].add(coarse_total)
    node_grad = node_sum.astype(jnp.bfloat16)
    return (node_grad, edge_grad, edge_upgrad, edge_downgrad, node_upgrad, node_downgrad, edge_gaingrad, node_gaingrad)
```

```python
import functools
import math

import jax
import jax.numpy as jnp
from jax import lax
from jax.experimental import pallas as pl
from jax.experimental.pallas import tpu as pltpu
from jax.sharding import PartitionSpec as P

EPSILON = 1e-05
BF16 = jnp.bfloat16
F32 = jnp.float32
MESH = pl.DeviceIdType.MESH
TILE = 16
BLOCK = 64


def last_dot(left, right):
    return lax.dot_general(left, right, (((1,), (1,)), ((), ())), preferred_element_type=F32)


def first_dot(left, right):
    return lax.dot_general(left, right, (((0,), (0,)), ((), ())), preferred_element_type=F32)


def onehot(index, count):
    rows = lax.broadcasted_iota(jnp.int32, (count, index.shape[1]), 0)
    return (rows == index).astype(F32).astype(BF16)


def norm_back(mixed, gain, upstream):
    centred = mixed - jnp.mean(mixed, -1, keepdims=True)
    inverse = lax.rsqrt(jnp.mean(centred * centred, -1, keepdims=True) + EPSILON)
    normed = centred * inverse
    scaled = upstream * gain
    delta = inverse * (
        scaled
        - jnp.mean(scaled, -1, keepdims=True)
        - normed * jnp.mean(scaled * normed, -1, keepdims=True)
    )
    return delta, normed


def stages_of(sizes):
    found = []
    for axis in ("dp", "space"):
        step = 1
        while step < sizes[axis]:
            found.append((axis, step))
            step *= 2
    return found


def halving_rows(rows, count):
    plan = []
    for _ in range(count):
        halves = (rows // 2) % TILE == 0
        rows = rows // 2 if halves else rows
        plan.append((rows, halves))
    return plan


def kernel(
    sizes,
    edge_scale,
    node_scale,
    node_latent,
    halo_latent,
    coarse_latent,
    edge_latent,
    edge_preact,
    edge_mixed,
    node_message,
    node_preact,
    node_mixed,
    edge_cotangent,
    node_cotangent,
    senders,
    receivers,
    send_rows,
    coarse_rows,
    edge_up,
    edge_down,
    edge_gain,
    node_up,
    node_down,
    node_gain,
    node_grad,
    edge_grad,
    edge_upgrad,
    edge_downgrad,
    node_upgrad,
    node_downgrad,
    edge_gaingrad,
    node_gaingrad,
    node_delta,
    node_hidden,
    node_signal,
    edge_delta,
    edge_hidden,
    edge_signal,
    edge_slope,
    sender_latent,
    receiver_latent,
    gathered,
    gain_sums,
    messages,
    edge_sent,
    edge_got,
    ext_own,
    ext_sent,
    ext_got,
    halo_sent,
    halo_got,
    coarse_sent,
    coarse_got,
    up_total,
    up_sent,
    up_got,
    down_total,
    down_sent,
    down_got,
    gain_sent,
    gain_got,
    sum_send,
    sum_recv,
    mp_send,
    mp_recv,
    halo_send,
    halo_recv,
    coarse_send,
    coarse_recv,
):
    mp, regions = sizes["mp"], sizes["space"]
    width = node_latent.shape[2]
    nodes = node_latent.shape[1]
    edges = edge_latent.shape[1]
    halo = halo_latent.shape[1] // 2
    coarse = coarse_latent.shape[1]
    owned = coarse // regions
    quarter = width // mp
    region = lax.axis_index("space")
    feature = lax.axis_index("mp")
    stages = stages_of(sizes)

    def beside(axis, shift):
        return lax.rem(lax.axis_index(axis) + shift, sizes[axis])

    barrier = pltpu.get_barrier_semaphore()
    for axis in ("mp", "dp", "space"):
        for shift in range(1, sizes[axis]):
            pl.semaphore_signal(
                barrier, inc=1, device_id={axis: beside(axis, shift)}, device_id_type=MESH
            )

    def remote(source, target, send, recv, axis, place):
        return pltpu.make_async_remote_copy(
            src_ref=source,
            dst_ref=target,
            send_sem=send,
            recv_sem=recv,
            device_id={axis: place},
            device_id_type=MESH,
        )

    def partner_of(axis, step):
        mine = lax.axis_index(axis)
        bit = lax.rem(mine // step, 2)
        return bit, mine + step - 2 * step * bit

    def summed(slot, total, sent, got, out, base, scale):
        rows = total.shape[0]
        start, held, filled = jnp.int32(0), rows, 0
        back = []
        for number, (axis, step) in enumerate(stages):
            count, halves = halving_rows(rows, len(stages))[number]
            bit, partner = partner_of(axis, step)
            place = pl.ds(filled, count)
            if halves:
                keep, give = start + bit * count, start + (1 - bit) * count
            else:
                keep = give = start
            keep, give = pl.multiple_of(keep, count), pl.multiple_of(give, count)
            sent[place, :] = total[pl.ds(give, count), :].astype(BF16)
            copy = remote(
                sent.at[place],
                got.at[place],
                sum_send.at[slot, number],
                sum_recv.at[slot, number],
                axis,
                partner,
            )
            copy.start()
            yield
            copy.wait()
            if halves:
                mine = total[pl.ds(keep, count), :]
                back.append((number, axis, partner, start))
            else:
                mine = sent[place, :].astype(F32)
            total[pl.ds(keep, count), :] = mine + got[place, :].astype(F32)
            start, held, filled = keep, count, filled + count
        final = pl.ds(pl.multiple_of(base + start, held), held)
        out[final, :] = (total[pl.ds(start, held), :] * scale).astype(BF16)
        for number, axis, partner, before in reversed(back):
            place = pl.ds(pl.multiple_of(base + start, held), held)
            copy = remote(
                out.at[place],
                out.at[place],
                sum_send.at[slot, len(stages) + number],
                sum_recv.at[slot, len(stages) + number],
                axis,
                partner,
            )
            copy.start()
            yield
            copy.wait()
            start, held = before, 2 * held

    def summed_gains(slot):
        value = gain_sums[...]
        for number, (axis, step) in enumerate(stages):
            _, partner = partner_of(axis, step)
            gain_sent[number] = value
            copy = remote(
                gain_sent.at[number],
                gain_got.at[number],
                sum_send.at[slot, number],
                sum_recv.at[slot, number],
                axis,
                partner,
            )
            copy.start()
            yield
            copy.wait()
            value = value + gain_got[number]
        edge_gaingrad[...] = value[0:1] * edge_scale
        node_gaingrad[...] = value[1:2] * node_scale

    running = []

    def begin(steps):
        next(steps)
        running.append(steps)

    def advance(times=1):
        for _ in range(times):
            for steps in list(running):
                if next(steps, "done") == "done":
                    running.remove(steps)

    def up_chunk(slot, value, out, base, scale):
        up_total[slot] = value
        begin(
            summed(slot, up_total.at[slot], up_sent.at[slot], up_got.at[slot], out, base, scale)
        )

    def down_chunk(slot, value, out, scale):
        down_total[slot] = value
        begin(
            summed(
                5 + slot, down_total.at[slot], down_sent.at[slot], down_got.at[slot], out, 0, scale
            )
        )

    gain_sums[...] = jnp.zeros_like(gain_sums)

    def node_rows(number, _):
        rows = pl.ds(pl.multiple_of(number * BLOCK, BLOCK), BLOCK)
        upstream = node_cotangent[0, rows, :].astype(F32)
        delta, normed = norm_back(node_mixed[0, rows, :].astype(F32), node_gain[...], upstream)
        gain_sums[1:2, :] += jnp.sum(upstream * normed, 0, keepdims=True)
        delta = delta.astype(BF16)
        node_delta[rows, :] = delta
        act = node_preact[0, rows, :].astype(F32)
        logistic = jax.nn.sigmoid(act)
        node_hidden[rows, :] = (act * logistic).astype(BF16)
        slope = logistic * (1.0 + act * (1.0 - logistic))
        node_signal[rows, :] = (last_dot(delta, node_down[...]) * slope).astype(BF16)
        return 0

    lax.fori_loop(0, nodes // BLOCK, node_rows, 0)
    messages[feature] = last_dot(node_signal[...], node_up[width:, :]).astype(BF16)

    pl.semaphore_wait(barrier, (mp - 1) + (sizes["dp"] - 1) + (regions - 1))
    message_copies = []
    for shift in range(1, mp):
        copy = remote(
            messages.at[feature],
            messages.at[feature],
            mp_send.at[0, shift],
            mp_recv.at[0, shift],
            "mp",
            beside("mp", shift),
        )
        copy.start()
        message_copies.append(copy)

    down_chunk(1, first_dot(node_hidden[...], node_delta[...]), node_downgrad, node_scale)
    up_chunk(3, first_dot(node_latent[0], node_signal[...]), node_upgrad, 0, node_scale)
    up_chunk(4, first_dot(node_message[0], node_signal[...]), node_upgrad, width, node_scale)

    receiver_hot = onehot(receivers[...], nodes)
    sender_hot = onehot(senders[...], nodes + 2 * halo + coarse)
    advance()

    def edge_acts(number, _):
        rows = pl.ds(pl.multiple_of(number * BLOCK, BLOCK), BLOCK)
        act = edge_preact[0, rows, :].astype(F32)
        logistic = jax.nn.sigmoid(act)
        edge_hidden[rows, :] = (act * logistic).astype(BF16)
        edge_slope[rows, :] = logistic * (1.0 + act * (1.0 - logistic))
        return 0

    lax.fori_loop(0, edges // BLOCK, edge_acts, 0)
    advance()
    receiver_latent[...] = first_dot(receiver_hot, node_latent[0]).astype(BF16)
    extended = jnp.concatenate([node_latent[0], halo_latent[0], coarse_latent[0]], 0)
    sender_latent[...] = first_dot(sender_hot, extended).astype(BF16)
    advance()

    for copy in message_copies:
        copy.wait()
    message = messages[0].astype(F32)
    for slot in range(1, mp):
        message = message + messages[slot].astype(F32)
    gathered[...] = first_dot(receiver_hot, message.astype(BF16))

    def edge_rows(number, _):
        rows = pl.ds(pl.multiple_of(number * BLOCK, BLOCK), BLOCK)
        upstream = edge_cotangent[0, rows, :].astype(F32) + gathered[rows, :]
        delta, normed = norm_back(edge_mixed[0, rows, :].astype(F32), edge_gain[...], upstream)
        gain_sums[0:1, :] += jnp.sum(upstream * normed, 0, keepdims=True)
        delta = delta.astype(BF16)
        edge_delta[rows, :] = delta
        edge_signal[rows, :] = (last_dot(delta, edge_down[...]) * edge_slope[rows, :]).astype(BF16)
        return 0

    lax.fori_loop(0, edges // BLOCK, edge_rows, 0)
    advance()
    down_chunk(0, first_dot(edge_hidden[...], edge_delta[...]), edge_downgrad, edge_scale)

    def weight_rows(block, place):
        return pl.ds(pl.multiple_of(block * width + place * quarter, quarter), quarter)

    def ext_part(place):
        signal = edge_signal[...]
        from_senders = last_dot(signal, edge_up[weight_rows(1, place), :]).astype(BF16)
        from_receivers = last_dot(signal, edge_up[weight_rows(2, place), :]).astype(BF16)
        ext = jnp.dot(sender_hot, from_senders, preferred_element_type=F32)
        node = jnp.dot(receiver_hot, from_receivers, preferred_element_type=F32)
        node = node + last_dot(node_signal[...], node_up[weight_rows(0, place), :])
        return ext[:nodes] + node, ext[nodes:]

    ext_copies, edge_copies = [], []
    for shift in range(1, mp):
        place = beside("mp", shift)
        node, ext = ext_part(place)
        ext_sent[shift, :nodes, :] = node.astype(BF16)
        ext_sent[shift, nodes:, :] = ext.astype(BF16)
        copy = remote(
            ext_sent.at[shift],
            ext_got.at[shift],
            mp_send.at[1, shift],
            mp_recv.at[1, shift],
            "mp",
            place,
        )
        copy.start()
        ext_copies.append(copy)
    up_chunk(0, first_dot(edge_latent[0], edge_signal[...]), edge_upgrad, 0, edge_scale)
    up_chunk(1, first_dot(sender_latent[...], edge_signal[...]), edge_upgrad, width, edge_scale)
    up_chunk(
        2, first_dot(receiver_latent[...], edge_signal[...]), edge_upgrad, 2 * width, edge_scale
    )
    begin(summed_gains(7))
    advance()
    for shift in range(1, mp):
        place = beside("mp", shift)
        part = last_dot(edge_signal[...], edge_up[weight_rows(0, place), :])
        edge_sent[shift] = part.astype(BF16)
        copy = remote(
            edge_sent.at[shift],
            edge_got.at[shift],
            mp_send.at[2, shift],
            mp_recv.at[2, shift],
            "mp",
            place,
        )
        copy.start()
        edge_copies.append(copy)
    node, ext = ext_part(feature)
    ext_own[:nodes, :] = node
    ext_own[nodes:, :] = ext
    advance()

    for copy in ext_copies:
        copy.wait()
    ext = ext_own[nodes:, :]
    for shift in range(1, mp):
        ext = ext + ext_got[shift, nodes:, :].astype(F32)
    halo_sent[...] = ext[: 2 * halo].astype(BF16)
    coarse_sent[...] = ext[2 * halo :]
    far_copies = []
    for slot, shift in enumerate((regions - 1, 1)):
        rows = pl.ds(slot * halo, halo)
        copy = remote(
            halo_sent.at[rows],
            halo_got.at[rows],
            halo_send.at[slot],
            halo_recv.at[slot],
            "space",
            beside("space", shift),
        )
        copy.start()
        far_copies.append(copy)
    for shift in range(1, regions):
        place = beside("space", shift)
        rows = pl.ds(pl.multiple_of(place * owned, owned), owned)
        copy = remote(
            coarse_sent.at[rows],
            coarse_got.at[shift],
            coarse_send.at[shift],
            coarse_recv.at[shift],
            "space",
            place,
        )
        copy.start()
        far_copies.append(copy)
    advance()

    columns = pl.ds(pl.multiple_of(feature * quarter, quarter), quarter)
    part = last_dot(edge_signal[...], edge_up[weight_rows(0, feature), :])
    part = part + edge_cotangent[0, :, columns].astype(F32)
    for copy in edge_copies:
        copy.wait()
    for shift in range(1, mp):
        part = part + edge_got[shift].astype(F32)
    edge_grad[0] = part.astype(BF16)
    advance()

    total = ext_own[:nodes, :] + node_cotangent[0, :, columns].astype(F32)
    for shift in range(1, mp):
        total = total + ext_got[shift, :nodes, :].astype(F32)
    for copy in far_copies:
        copy.wait()
    total = total + jnp.dot(
        onehot(send_rows[...], nodes), halo_got[...], preferred_element_type=F32
    )
    own_coarse = coarse_sent[pl.ds(pl.multiple_of(region * owned, owned), owned), :]
    for shift in range(1, regions):
        own_coarse = own_coarse + coarse_got[shift]
    own_coarse = jnp.concatenate([own_coarse.astype(BF16).astype(F32)] * regions, 0).astype(BF16)
    owner = lax.broadcasted_iota(jnp.int32, (1, coarse), 1) // owned
    coarse_hot = onehot(jnp.where(owner == region, coarse_rows[...], -1), nodes)
    total = total + jnp.dot(coarse_hot, own_coarse, preferred_element_type=F32)
    node_grad[0] = total.astype(BF16)
    while running:
        advance()


def body(sizes, *arguments):
    (node_latent, halo_latent, coarse_latent, edge_latent, edge_preact) = arguments[:5]
    senders, receivers, send_rows, coarse_rows = arguments[11:15]
    edge_up, edge_down, edge_gain, node_up, node_down, node_gain = arguments[15:]
    width = node_latent.shape[2]
    nodes = node_latent.shape[1]
    edges = edge_latent.shape[1]
    halo_rows = halo_latent.shape[1]
    coarse = coarse_latent.shape[1]
    hidden = edge_preact.shape[2]
    mp, regions = sizes["mp"], sizes["space"]
    quarter = width // mp
    owned = coarse // regions
    extended = nodes + halo_rows + coarse
    stages = len(stages_of(sizes))
    samples = node_latent.shape[0] * sizes["dp"]
    edge_scale = 1.0 / math.sqrt(samples * edges * regions)
    node_scale = 1.0 / math.sqrt(samples * nodes * regions)
    up_rows = sum(rows for rows, _ in halving_rows(width, stages))
    down_rows = sum(rows for rows, _ in halving_rows(hidden, stages))
    shape = jax.ShapeDtypeStruct
    vmem = pltpu.VMEM
    semaphores = pltpu.SemaphoreType.DMA
    out_shape = (
        shape((1, nodes, quarter), BF16),
        shape((1, edges, quarter), BF16),
        shape((3 * width, hidden), BF16),
        shape((hidden, width), BF16),
        shape((2 * width, hidden), BF16),
        shape((hidden, width), BF16),
        shape((1, width), F32),
        shape((1, width), F32),
    )
    scratch = [
        vmem((nodes, width), BF16),
        vmem((nodes, hidden), BF16),
        vmem((nodes, hidden), BF16),
        vmem((edges, width), BF16),
        vmem((edges, hidden), BF16),
        vmem((edges, hidden), BF16),
        vmem((edges, hidden), F32),
        vmem((edges, width), BF16),
        vmem((edges, width), BF16),
        vmem((edges, width), F32),
        vmem((8, width), F32),
        vmem((mp, nodes, width), BF16),
        vmem((mp, edges, quarter), BF16),
        vmem((mp, edges, quarter), BF16),
        vmem((extended, quarter), F32),
        vmem((mp, extended, quarter), BF16),
        vmem((mp, extended, quarter), BF16),
        vmem((halo_rows, quarter), BF16),
        vmem((halo_rows, quarter), BF16),
        vmem((coarse, quarter), F32),
        vmem((regions, owned, quarter), F32),
        vmem((5, width, hidden), F32),
        vmem((5, up_rows, hidden), BF16),
        vmem((5, up_rows, hidden), BF16),
        vmem((2, hidden, width), F32),
        vmem((2, down_rows, width), BF16),
        vmem((2, down_rows, width), BF16),
        vmem((stages, 8, width), F32),
        vmem((stages, 8, width), F32),
        semaphores((8, 2 * stages)),
        semaphores((8, 2 * stages)),
        semaphores((3, mp)),
        semaphores((3, mp)),
        semaphores((2,)),
        semaphores((2,)),
        semaphores((regions,)),
        semaphores((regions,)),
    ]
    operands = arguments[:11] + (
        senders.reshape(1, -1),
        receivers.reshape(1, -1),
        send_rows.reshape(1, -1),
        coarse_rows.reshape(1, -1),
        edge_up,
        edge_down,
        edge_gain.reshape(1, -1),
        node_up,
        node_down,
        node_gain.reshape(1, -1),
    )
    outs = pl.pallas_call(
        functools.partial(kernel, sizes, edge_scale, node_scale),
        out_shape=out_shape,
        in_specs=[pl.BlockSpec(memory_space=vmem)] * len(operands),
        out_specs=tuple([pl.BlockSpec(memory_space=vmem)] * len(out_shape)),
        scratch_shapes=scratch,
        compiler_params=pltpu.CompilerParams(
            collective_id=0, has_side_effects=True, vmem_limit_bytes=56 * 1024 * 1024
        ),
    )(*operands)
    return outs[:6] + (outs[6].reshape(-1), outs[7].reshape(-1))


def solution(mesh):
    sizes = {axis: mesh.shape[axis] for axis in ("space", "dp", "mp")}
    return jax.shard_map(
        functools.partial(body, sizes),
        mesh=mesh,
        in_specs=(
            P(("group", "dp"), "space", None),
            P(("group", "dp"), "space", None),
            P(("group", "dp"), None, None),
            P(("group", "dp"), "space", None),
            P(("group", "dp"), "space", "mp"),
            P(("group", "dp"), "space", None),
            P(("group", "dp"), "space", None),
            P(("group", "dp"), "space", "mp"),
            P(("group", "dp"), "space", None),
            P(("group", "dp"), "space", None),
            P(("group", "dp"), "space", None),
            P("space"),
            P("space"),
            P("space", None, None),
            P(),
            P(None, "mp"),
            P("mp", None),
            P(),
            P(None, "mp"),
            P("mp", None),
            P(),
        ),
        out_specs=(
            P(("group", "dp"), "space", "mp"),
            P(("group", "dp"), "space", "mp"),
            P("group", "mp"),
            P(("group", "mp"), None),
            P("group", "mp"),
            P(("group", "mp"), None),
            P("group"),
            P("group"),
        ),
        check_vma=False,
    )
```

```python
import functools
import math

import jax
import jax.numpy as jnp
from jax import lax
from jax.experimental import pallas as pl
from jax.experimental.pallas import tpu as pltpu
from jax.sharding import PartitionSpec as P

EPSILON = 1e-05
BF16 = jnp.bfloat16
F32 = jnp.float32
MESH = pl.DeviceIdType.MESH
TILE = 16
BLOCK = 64


def last_dot(left, right):
    return lax.dot_general(left, right, (((1,), (1,)), ((), ())), preferred_element_type=F32)


def first_dot(left, right):
    return lax.dot_general(left, right, (((0,), (0,)), ((), ())), preferred_element_type=F32)


def onehot(index, count):
    rows = lax.broadcasted_iota(jnp.int32, (count, index.shape[1]), 0)
    return (rows == index).astype(F32).astype(BF16)


def norm_back(mixed, gain, upstream):
    centred = mixed - jnp.mean(mixed, -1, keepdims=True)
    inverse = lax.rsqrt(jnp.mean(centred * centred, -1, keepdims=True) + EPSILON)
    normed = centred * inverse
    scaled = upstream * gain
    delta = inverse * (
        scaled
        - jnp.mean(scaled, -1, keepdims=True)
        - normed * jnp.mean(scaled * normed, -1, keepdims=True)
    )
    return delta, normed


def stages_of(sizes):
    found = []
    for axis in ("dp", "space"):
        step = 1
        while step < sizes[axis]:
            found.append((axis, step))
            step *= 2
    return found


def halving_rows(rows, count):
    plan = []
    for _ in range(count):
        halves = (rows // 2) % TILE == 0
        rows = rows // 2 if halves else rows
        plan.append((rows, halves))
    return plan


ORDER = (
    "node_mixed",
    "node_cotangent",
    "node_gain",
    "node_preact",
    "node_down",
    "node_up",
    "node_latent",
    "node_message",
    "receivers",
    "senders",
    "edge_preact",
    "halo_latent",
    "coarse_latent",
    "edge_cotangent",
    "edge_mixed",
    "edge_gain",
    "edge_down",
    "edge_up",
    "edge_latent",
    "send_rows",
    "coarse_rows",
)


def staged_kernel(sizes, edge_scale, node_scale, inputs, *refs):
    places = refs[-inputs:]
    kernel(sizes, edge_scale, node_scale, refs[:inputs], *places, *refs[inputs:-inputs])


def kernel(
    sizes,
    edge_scale,
    node_scale,
    operands,
    node_latent,
    halo_latent,
    coarse_latent,
    edge_latent,
    edge_preact,
    edge_mixed,
    node_message,
    node_preact,
    node_mixed,
    edge_cotangent,
    node_cotangent,
    senders,
    receivers,
    send_rows,
    coarse_rows,
    edge_up,
    edge_down,
    edge_gain,
    node_up,
    node_down,
    node_gain,
    node_grad,
    edge_grad,
    edge_upgrad,
    edge_downgrad,
    node_upgrad,
    node_downgrad,
    edge_gaingrad,
    node_gaingrad,
    node_delta,
    node_hidden,
    node_signal,
    edge_delta,
    edge_hidden,
    edge_signal,
    edge_slope,
    sender_latent,
    receiver_latent,
    gathered,
    gain_sums,
    messages,
    edge_sent,
    edge_got,
    ext_own,
    ext_sent,
    ext_got,
    halo_sent,
    halo_got,
    coarse_sent,
    coarse_got,
    up_total,
    up_sent,
    up_got,
    down_total,
    down_sent,
    down_got,
    gain_sent,
    gain_got,
    sum_send,
    sum_recv,
    mp_send,
    mp_recv,
    halo_send,
    halo_recv,
    coarse_send,
    coarse_recv,
    load_sem,
):
    mp, regions = sizes["mp"], sizes["space"]
    held = {
        "node_latent": node_latent,
        "halo_latent": halo_latent,
        "coarse_latent": coarse_latent,
        "edge_latent": edge_latent,
        "edge_preact": edge_preact,
        "edge_mixed": edge_mixed,
        "node_message": node_message,
        "node_preact": node_preact,
        "node_mixed": node_mixed,
        "edge_cotangent": edge_cotangent,
        "node_cotangent": node_cotangent,
        "senders": senders,
        "receivers": receivers,
        "send_rows": send_rows,
        "coarse_rows": coarse_rows,
        "edge_up": edge_up,
        "edge_down": edge_down,
        "edge_gain": edge_gain,
        "node_up": node_up,
        "node_down": node_down,
        "node_gain": node_gain,
    }
    loads = {
        name: pltpu.make_async_copy(operands[place], held[name], load_sem.at[place])
        for place, name in enumerate(held)
    }
    for name in ORDER:
        loads[name].start()

    def ready(*names):
        for name in names:
            loads.pop(name).wait()

    width = node_latent.shape[2]
    nodes = node_latent.shape[1]
    edges = edge_latent.shape[1]
    halo = halo_latent.shape[1] // 2
    coarse = coarse_latent.shape[1]
    owned = coarse // regions
    quarter = width // mp
    region = lax.axis_index("space")
    feature = lax.axis_index("mp")
    stages = stages_of(sizes)

    def beside(axis, shift):
        return lax.rem(lax.axis_index(axis) + shift, sizes[axis])

    barrier = pltpu.get_barrier_semaphore()
    for axis in ("mp", "dp", "space"):
        for shift in range(1, sizes[axis]):
            pl.semaphore_signal(
                barrier, inc=1, device_id={axis: beside(axis, shift)}, device_id_type=MESH
            )

    def remote(source, target, send, recv, axis, place):
        return pltpu.make_async_remote_copy(
            src_ref=source,
            dst_ref=target,
            send_sem=send,
            recv_sem=recv,
            device_id={axis: place},
            device_id_type=MESH,
        )

    def partner_of(axis, step):
        mine = lax.axis_index(axis)
        bit = lax.rem(mine // step, 2)
        return bit, mine + step - 2 * step * bit

    def summed(slot, total, sent, got, out, base, scale):
        rows = total.shape[0]
        start, held, filled = jnp.int32(0), rows, 0
        back = []
        for number, (axis, step) in enumerate(stages):
            count, halves = halving_rows(rows, len(stages))[number]
            bit, partner = partner_of(axis, step)
            place = pl.ds(filled, count)
            if halves:
                keep, give = start + bit * count, start + (1 - bit) * count
            else:
                keep = give = start
            keep, give = pl.multiple_of(keep, count), pl.multiple_of(give, count)
            sent[place, :] = total[pl.ds(give, count), :].astype(BF16)
            copy = remote(
                sent.at[place],
                got.at[place],
                sum_send.at[slot, number],
                sum_recv.at[slot, number],
                axis,
                partner,
            )
            copy.start()
            yield
            copy.wait()
            if halves:
                mine = total[pl.ds(keep, count), :]
                back.append((number, axis, partner, start))
            else:
                mine = sent[place, :].astype(F32)
            total[pl.ds(keep, count), :] = mine + got[place, :].astype(F32)
            start, held, filled = keep, count, filled + count
        final = pl.ds(pl.multiple_of(base + start, held), held)
        out[final, :] = (total[pl.ds(start, held), :] * scale).astype(BF16)
        for number, axis, partner, before in reversed(back):
            place = pl.ds(pl.multiple_of(base + start, held), held)
            copy = remote(
                out.at[place],
                out.at[place],
                sum_send.at[slot, len(stages) + number],
                sum_recv.at[slot, len(stages) + number],
                axis,
                partner,
            )
            copy.start()
            yield
            copy.wait()
            start, held = before, 2 * held

    def summed_gains(slot):
        value = gain_sums[...]
        for number, (axis, step) in enumerate(stages):
            _, partner = partner_of(axis, step)
            gain_sent[number] = value
            copy = remote(
                gain_sent.at[number],
                gain_got.at[number],
                sum_send.at[slot, number],
                sum_recv.at[slot, number],
                axis,
                partner,
            )
            copy.start()
            yield
            copy.wait()
            value = value + gain_got[number]
        edge_gaingrad[...] = value[0:1] * edge_scale
        node_gaingrad[...] = value[1:2] * node_scale

    running = []

    def begin(steps):
        next(steps)
        running.append(steps)

    def advance(times=1):
        for _ in range(times):
            for steps in list(running):
                if next(steps, "done") == "done":
                    running.remove(steps)

    def up_chunk(slot, value, out, base, scale):
        up_total[slot] = value
        begin(
            summed(slot, up_total.at[slot], up_sent.at[slot], up_got.at[slot], out, base, scale)
        )

    def down_chunk(slot, value, out, scale):
        down_total[slot] = value
        begin(
            summed(
                5 + slot, down_total.at[slot], down_sent.at[slot], down_got.at[slot], out, 0, scale
            )
        )

    gain_sums[...] = jnp.zeros_like(gain_sums)

    ready("node_mixed", "node_cotangent", "node_gain", "node_preact", "node_down")

    def node_rows(number, _):
        rows = pl.ds(pl.multiple_of(number * BLOCK, BLOCK), BLOCK)
        upstream = node_cotangent[0, rows, :].astype(F32)
        delta, normed = norm_back(node_mixed[0, rows, :].astype(F32), node_gain[...], upstream)
        gain_sums[1:2, :] += jnp.sum(upstream * normed, 0, keepdims=True)
        delta = delta.astype(BF16)
        node_delta[rows, :] = delta
        act = node_preact[0, rows, :].astype(F32)
        logistic = jax.nn.sigmoid(act)
        node_hidden[rows, :] = (act * logistic).astype(BF16)
        slope = logistic * (1.0 + act * (1.0 - logistic))
        node_signal[rows, :] = (last_dot(delta, node_down[...]) * slope).astype(BF16)
        return 0

    lax.fori_loop(0, nodes // BLOCK, node_rows, 0)
    ready("node_up")
    messages[feature] = last_dot(node_signal[...], node_up[width:, :]).astype(BF16)

    pl.semaphore_wait(barrier, (mp - 1) + (sizes["dp"] - 1) + (regions - 1))
    message_copies = []
    for shift in range(1, mp):
        copy = remote(
            messages.at[feature],
            messages.at[feature],
            mp_send.at[0, shift],
            mp_recv.at[0, shift],
            "mp",
            beside("mp", shift),
        )
        copy.start()
        message_copies.append(copy)

    ready("node_latent", "node_message")
    down_chunk(1, first_dot(node_hidden[...], node_delta[...]), node_downgrad, node_scale)
    up_chunk(3, first_dot(node_latent[0], node_signal[...]), node_upgrad, 0, node_scale)
    up_chunk(4, first_dot(node_message[0], node_signal[...]), node_upgrad, width, node_scale)

    ready("senders", "receivers", "edge_preact", "halo_latent", "coarse_latent")
    receiver_hot = onehot(receivers[...], nodes)
    sender_hot = onehot(senders[...], nodes + 2 * halo + coarse)

    def edge_acts(number, _):
        rows = pl.ds(pl.multiple_of(number * BLOCK, BLOCK), BLOCK)
        act = edge_preact[0, rows, :].astype(F32)
        logistic = jax.nn.sigmoid(act)
        edge_hidden[rows, :] = (act * logistic).astype(BF16)
        edge_slope[rows, :] = logistic * (1.0 + act * (1.0 - logistic))
        return 0

    lax.fori_loop(0, edges // BLOCK, edge_acts, 0)
    advance()
    receiver_latent[...] = first_dot(receiver_hot, node_latent[0]).astype(BF16)
    extended = jnp.concatenate([node_latent[0], halo_latent[0], coarse_latent[0]], 0)
    sender_latent[...] = first_dot(sender_hot, extended).astype(BF16)

    ready(*tuple(loads))
    for copy in message_copies:
        copy.wait()
    message = messages[0].astype(F32)
    for slot in range(1, mp):
        message = message + messages[slot].astype(F32)
    gathered[...] = first_dot(receiver_hot, message.astype(BF16))
    advance()

    def edge_rows(number, _):
        rows = pl.ds(pl.multiple_of(number * BLOCK, BLOCK), BLOCK)
        upstream = edge_cotangent[0, rows, :].astype(F32) + gathered[rows, :]
        delta, normed = norm_back(edge_mixed[0, rows, :].astype(F32), edge_gain[...], upstream)
        gain_sums[0:1, :] += jnp.sum(upstream * normed, 0, keepdims=True)
        delta = delta.astype(BF16)
        edge_delta[rows, :] = delta
        edge_signal[rows, :] = (last_dot(delta, edge_down[...]) * edge_slope[rows, :]).astype(BF16)
        return 0

    lax.fori_loop(0, edges // BLOCK, edge_rows, 0)
    down_chunk(0, first_dot(edge_hidden[...], edge_delta[...]), edge_downgrad, edge_scale)

    def weight_rows(block, place):
        return pl.ds(pl.multiple_of(block * width + place * quarter, quarter), quarter)

    def ext_part(place):
        signal = edge_signal[...]
        from_senders = last_dot(signal, edge_up[weight_rows(1, place), :]).astype(BF16)
        from_receivers = last_dot(signal, edge_up[weight_rows(2, place), :]).astype(BF16)
        ext = jnp.dot(sender_hot, from_senders, preferred_element_type=F32)
        node = jnp.dot(receiver_hot, from_receivers, preferred_element_type=F32)
        node = node + last_dot(node_signal[...], node_up[weight_rows(0, place), :])
        return ext[:nodes] + node, ext[nodes:]

    ext_copies, edge_copies = [], []
    for shift in range(1, mp):
        place = beside("mp", shift)
        node, ext = ext_part(place)
        ext_sent[shift, :nodes, :] = node.astype(BF16)
        ext_sent[shift, nodes:, :] = ext.astype(BF16)
        copy = remote(
            ext_sent.at[shift],
            ext_got.at[shift],
            mp_send.at[1, shift],
            mp_recv.at[1, shift],
            "mp",
            place,
        )
        copy.start()
        ext_copies.append(copy)
    up_chunk(0, first_dot(edge_latent[0], edge_signal[...]), edge_upgrad, 0, edge_scale)
    up_chunk(1, first_dot(sender_latent[...], edge_signal[...]), edge_upgrad, width, edge_scale)
    up_chunk(
        2, first_dot(receiver_latent[...], edge_signal[...]), edge_upgrad, 2 * width, edge_scale
    )
    begin(summed_gains(7))
    for shift in range(1, mp):
        place = beside("mp", shift)
        part = last_dot(edge_signal[...], edge_up[weight_rows(0, place), :])
        edge_sent[shift] = part.astype(BF16)
        copy = remote(
            edge_sent.at[shift],
            edge_got.at[shift],
            mp_send.at[2, shift],
            mp_recv.at[2, shift],
            "mp",
            place,
        )
        copy.start()
        edge_copies.append(copy)
    node, ext = ext_part(feature)
    ext_own[:nodes, :] = node
    ext_own[nodes:, :] = ext
    advance(2)

    for copy in ext_copies:
        copy.wait()
    ext = ext_own[nodes:, :]
    for shift in range(1, mp):
        ext = ext + ext_got[shift, nodes:, :].astype(F32)
    halo_sent[...] = ext[: 2 * halo].astype(BF16)
    coarse_sent[...] = ext[2 * halo :]
    far_copies = []
    for slot, shift in enumerate((regions - 1, 1)):
        rows = pl.ds(slot * halo, halo)
        copy = remote(
            halo_sent.at[rows],
            halo_got.at[rows],
            halo_send.at[slot],
            halo_recv.at[slot],
            "space",
            beside("space", shift),
        )
        copy.start()
        far_copies.append(copy)
    for shift in range(1, regions):
        place = beside("space", shift)
        rows = pl.ds(pl.multiple_of(place * owned, owned), owned)
        copy = remote(
            coarse_sent.at[rows],
            coarse_got.at[shift],
            coarse_send.at[shift],
            coarse_recv.at[shift],
            "space",
            place,
        )
        copy.start()
        far_copies.append(copy)
    advance()

    columns = pl.ds(pl.multiple_of(feature * quarter, quarter), quarter)
    part = last_dot(edge_signal[...], edge_up[weight_rows(0, feature), :])
    part = part + edge_cotangent[0, :, columns].astype(F32)
    for copy in edge_copies:
        copy.wait()
    for shift in range(1, mp):
        part = part + edge_got[shift].astype(F32)
    edge_grad[0] = part.astype(BF16)
    advance()

    total = ext_own[:nodes, :] + node_cotangent[0, :, columns].astype(F32)
    for shift in range(1, mp):
        total = total + ext_got[shift, :nodes, :].astype(F32)
    for copy in far_copies:
        copy.wait()
    total = total + jnp.dot(
        onehot(send_rows[...], nodes), halo_got[...], preferred_element_type=F32
    )
    own_coarse = coarse_sent[pl.ds(pl.multiple_of(region * owned, owned), owned), :]
    for shift in range(1, regions):
        own_coarse = own_coarse + coarse_got[shift]
    own_coarse = jnp.concatenate([own_coarse.astype(BF16).astype(F32)] * regions, 0).astype(BF16)
    owner = lax.broadcasted_iota(jnp.int32, (1, coarse), 1) // owned
    coarse_hot = onehot(jnp.where(owner == region, coarse_rows[...], -1), nodes)
    total = total + jnp.dot(coarse_hot, own_coarse, preferred_element_type=F32)
    node_grad[0] = total.astype(BF16)
    while running:
        advance()


def copy_kernel(*refs):
    count = len(refs) // 2
    sems = refs[-1]
    copies = [
        pltpu.make_async_copy(refs[place], refs[count + place], sems.at[place])
        for place in range(count)
    ]
    for copy in copies:
        copy.start()
    for copy in copies:
        copy.wait()


def copied(arrays):
    count = len(arrays)
    return pl.pallas_call(
        copy_kernel,
        out_shape=tuple(jax.ShapeDtypeStruct(array.shape, array.dtype) for array in arrays),
        in_specs=[pl.BlockSpec(memory_space=pltpu.VMEM)] * count,
        out_specs=tuple([pl.BlockSpec(memory_space=pl.ANY)] * count),
        scratch_shapes=[pltpu.SemaphoreType.DMA((count,))],
    )(*arrays)


def body(sizes, *arguments):
    (node_latent, halo_latent, coarse_latent, edge_latent, edge_preact) = arguments[:5]
    senders, receivers, send_rows, coarse_rows = arguments[11:15]
    edge_up, edge_down, edge_gain, node_up, node_down, node_gain = arguments[15:]
    width = node_latent.shape[2]
    nodes = node_latent.shape[1]
    edges = edge_latent.shape[1]
    halo_rows = halo_latent.shape[1]
    coarse = coarse_latent.shape[1]
    hidden = edge_preact.shape[2]
    mp, regions = sizes["mp"], sizes["space"]
    quarter = width // mp
    owned = coarse // regions
    extended = nodes + halo_rows + coarse
    stages = len(stages_of(sizes))
    samples = node_latent.shape[0] * sizes["dp"]
    edge_scale = 1.0 / math.sqrt(samples * edges * regions)
    node_scale = 1.0 / math.sqrt(samples * nodes * regions)
    up_rows = sum(rows for rows, _ in halving_rows(width, stages))
    down_rows = sum(rows for rows, _ in halving_rows(hidden, stages))
    shape = jax.ShapeDtypeStruct
    vmem = pltpu.VMEM
    semaphores = pltpu.SemaphoreType.DMA
    out_shape = (
        shape((1, nodes, quarter), BF16),
        shape((1, edges, quarter), BF16),
        shape((3 * width, hidden), BF16),
        shape((hidden, width), BF16),
        shape((2 * width, hidden), BF16),
        shape((hidden, width), BF16),
        shape((1, width), F32),
        shape((1, width), F32),
    )
    scratch = [
        vmem((nodes, width), BF16),
        vmem((nodes, hidden), BF16),
        vmem((nodes, hidden), BF16),
        vmem((edges, width), BF16),
        vmem((edges, hidden), BF16),
        vmem((edges, hidden), BF16),
        vmem((edges, hidden), F32),
        vmem((edges, width), BF16),
        vmem((edges, width), BF16),
        vmem((edges, width), F32),
        vmem((8, width), F32),
        vmem((mp, nodes, width), BF16),
        vmem((mp, edges, quarter), BF16),
        vmem((mp, edges, quarter), BF16),
        vmem((extended, quarter), F32),
        vmem((mp, extended, quarter), BF16),
        vmem((mp, extended, quarter), BF16),
        vmem((halo_rows, quarter), BF16),
        vmem((halo_rows, quarter), BF16),
        vmem((coarse, quarter), F32),
        vmem((regions, owned, quarter), F32),
        vmem((5, width, hidden), F32),
        vmem((5, up_rows, hidden), BF16),
        vmem((5, up_rows, hidden), BF16),
        vmem((2, hidden, width), F32),
        vmem((2, down_rows, width), BF16),
        vmem((2, down_rows, width), BF16),
        vmem((stages, 8, width), F32),
        vmem((stages, 8, width), F32),
        semaphores((8, 2 * stages)),
        semaphores((8, 2 * stages)),
        semaphores((3, mp)),
        semaphores((3, mp)),
        semaphores((2,)),
        semaphores((2,)),
        semaphores((regions,)),
        semaphores((regions,)),
        semaphores((len(ORDER),)),
    ]
    operands = arguments[:11] + (
        senders.reshape(1, -1),
        receivers.reshape(1, -1),
        send_rows.reshape(1, -1),
        coarse_rows.reshape(1, -1),
        edge_up,
        edge_down,
        edge_gain.reshape(1, -1),
        node_up,
        node_down,
        node_gain.reshape(1, -1),
    )
    outs = pl.pallas_call(
        functools.partial(staged_kernel, sizes, edge_scale, node_scale, len(operands)),
        out_shape=out_shape,
        in_specs=[pl.BlockSpec(memory_space=pl.ANY)] * len(operands),
        out_specs=tuple([pl.BlockSpec(memory_space=vmem)] * len(out_shape)),
        scratch_shapes=scratch + [vmem(array.shape, array.dtype) for array in operands],
        compiler_params=pltpu.CompilerParams(
            collective_id=0, has_side_effects=True, vmem_limit_bytes=56 * 1024 * 1024
        ),
    )(*operands)
    outs = copied(outs)
    return tuple(outs[:6]) + (outs[6].reshape(-1), outs[7].reshape(-1))


def solution(mesh):
    sizes = {axis: mesh.shape[axis] for axis in ("space", "dp", "mp")}
    return jax.shard_map(
        functools.partial(body, sizes),
        mesh=mesh,
        in_specs=(
            P(("group", "dp"), "space", None),
            P(("group", "dp"), "space", None),
            P(("group", "dp"), None, None),
            P(("group", "dp"), "space", None),
            P(("group", "dp"), "space", "mp"),
            P(("group", "dp"), "space", None),
            P(("group", "dp"), "space", None),
            P(("group", "dp"), "space", "mp"),
            P(("group", "dp"), "space", None),
            P(("group", "dp"), "space", None),
            P(("group", "dp"), "space", None),
            P("space"),
            P("space"),
            P("space", None, None),
            P(),
            P(None, "mp"),
            P("mp", None),
            P(),
            P(None, "mp"),
            P("mp", None),
            P(),
        ),
        out_specs=(
            P(("group", "dp"), "space", "mp"),
            P(("group", "dp"), "space", "mp"),
            P("group", "mp"),
            P(("group", "mp"), None),
            P("group", "mp"),
            P(("group", "mp"), None),
            P("group"),
            P("group"),
        ),
        check_vma=False,
    )
```
